32 devices in a mesh: ra: 8 (over z, core), dec: 4 (over y, x).
Axes of the slice: x: 2, y: 2, z: 4, core: 2. Of those that a mesh axis runs over, the one named last changes fastest.
Arguments:
- template: float32 [1024, 8192], P('dec', 'ra'), may hold values from -9 to 9
- science: float32 [1024, 8192], P('dec', 'ra'), may hold values from -12 to 12
- offsets: int32 [8, 4], P('ra', 'dec'), may hold values from 0 to 512, as said below
- source_dest: int32 [1024, 1], P(('ra', 'dec')), may hold values from 0 to 31; in each aligned block of 32 rows (0 to 31, 32 to 63, ...) at most 2 rows name the same one
- source_row: int32 [1024], P(('ra', 'dec')), may hold values from 0 to 192
- source_col: int32 [1024], P(('ra', 'dec')), may hold values from 0 to 960
Outputs:
- difference: float32 [1024, 8192], P('dec', 'ra')
- stamps: bfloat16 [32, 32, 2, 4096], P(('ra', 'dec'))
The draws below stay inside these ranges and needn't reach their ends.
Inputs may be any that keep to these rules, and one draw needn't show every extreme that they name: `offsets`: some tile has offset 512 in every draw, and at every ra index some band has offset 0. `source_dest`: the owner is a device number in the order of the sources; at most 2 sources of one tile name the same owner, and some tile sends 2 to one owner.
All inputs are finite; a program needn't handle non-finite values.
Results may differ from the reference program's by a relative error of at most 0.001.
Values may be sent and summed in bfloat16 or wider, within the bound.
A program may use at most 192 MiB of HBM per device.

```python
import math
import jax
import jax.numpy as jnp
import numpy as np
from jax import lax

ROWS = 256
COLS = 1024
MARGIN = 15
CUT = 64
CAP = 2
OFFMAX = 512
NSRC = 32
SOURCES = 1024
NY = 1024
NX = 8192
N_RA = 8
N_DEC = 4
DEVICES = 32


def offset_table(key):
    base = jax.random.fold_in(key, 4101)
    key_values, key_pick, key_zero = jax.random.split(base, 3)
    tiles_ra = NX // COLS
    tiles_dec = NY // ROWS
    values = jax.random.randint(key_values, (tiles_ra, tiles_dec), 0, OFFMAX + 1)
    zero_band = jax.random.randint(key_zero, (tiles_ra,), 0, tiles_dec)
    band_index = jnp.arange(tiles_dec)[None, :]
    cycle_index = jnp.arange(tiles_ra)[:, None]
    values = jnp.where(band_index == zero_band[:, None], 0, values)
    chosen = jax.random.randint(key_pick, (), 0, tiles_ra)
    top_band = (zero_band[chosen] + 1) % tiles_dec
    values = jnp.where((cycle_index == chosen) & (band_index == top_band), OFFMAX, values)
    return values.astype(jnp.int32)


def template_field(key):
    base = jax.random.fold_in(key, 5203)
    key_field = jax.random.fold_in(base, 0)
    field = jnp.clip(jax.random.normal(key_field, (NY, NX), jnp.float32), -6.0, 6.0)
    return field


def tap_family(spread):
    tap_axis = jnp.arange(2 * MARGIN + 1, dtype=jnp.float32) - MARGIN
    profile = jnp.exp(-tap_axis * tap_axis / (2.0 * spread * spread))
    profile = profile / jnp.sum(profile)
    scaled = tap_axis / spread
    return (profile, profile * scaled, profile * scaled * scaled)


def along_cols(field, taps):
    total = jnp.zeros_like(field)
    for index in range(2 * MARGIN + 1):
        total = total + taps[index] * jnp.roll(field, MARGIN - index, axis=1)
    return total


def along_rows(field, taps):
    padded = jnp.pad(field, ((MARGIN, MARGIN), (0, 0)))
    total = jnp.zeros_like(field)
    for index in range(2 * MARGIN + 1):
        total = total + taps[index] * padded[index:index + NY]
    return total


def broad_response(field):
    narrow_p, narrow_one, narrow_two = tap_family(1.0)
    middle_p, middle_one, middle_two = tap_family(2.5)
    wide_p, wide_one, wide_two = tap_family(5.0)
    pairs = [(wide_p, wide_two), (wide_two, wide_p), (wide_p + 0.5 * wide_one, wide_one), (0.5 * middle_one, middle_p), (0.3 * narrow_one, narrow_one)]
    total = jnp.zeros_like(field)
    for row_taps, col_taps in pairs:
        total = total + along_rows(along_cols(field, col_taps), row_taps)
    return 3.0 * total


def draw_offsets(key, part):
    return offset_table(key)


def draw_template(key, part):
    return template_field(key)


def draw_science(key, part):
    table = offset_table(key)
    field = template_field(key)
    key_noise = jax.random.fold_in(key, 6307)
    columns = jnp.arange(NX, dtype=jnp.int32)
    rows_idx = jnp.arange(NY, dtype=jnp.int32)
    shift_cols = table[(columns // COLS)[None, :], (rows_idx // ROWS)[:, None]]
    source = (columns[None, :] + shift_cols) % NX
    moved = jnp.take_along_axis(field, source, axis=1)
    broad = jnp.take_along_axis(broad_response(field), source, axis=1)
    noise = jnp.clip(jax.random.normal(key_noise, (NY, NX), jnp.float32), -6.0, 6.0)
    return jnp.clip(0.6 * moved + broad + 0.4 * noise, -12.0, 12.0)


def touch_ends(drawn, stream_key, smallest, largest):
    index_at = [jax.random.randint(jax.random.fold_in(stream_key, axis), (), 0, length) for axis, length in enumerate(drawn.shape)]
    longest = drawn.shape.index(max(drawn.shape))
    next_to = index_at[:longest] + [(index_at[longest] + 1) % drawn.shape[longest]] + index_at[longest + 1:]
    return drawn.at[tuple(index_at)].set(smallest).at[tuple(next_to)].set(largest)


def routed_block(rng, own, number, rows, amount, top, most, skew):
    ranking = jax.random.permutation(rng, amount)
    heavy_load, common = load_shares(amount, rows * top, most, skew, True), load_shares(amount, rows * top, most, skew, False)
    places = jnp.arange(amount)

    def named(tallies, offset_by):
        used = int((tallies > 0).sum())
        fixed = max(1, used // 4)
        shifted = fixed + (places - fixed + offset_by * (used - fixed)) % max(1, amount - fixed)
        return jnp.zeros((amount,), jnp.int32).at[ranking[jnp.where(places < fixed, places, shifted)]].set(jnp.asarray(tallies, jnp.int32))

    tallies = jnp.where(number % 4 == 0, named(heavy_load, number // 4), named(common, number - number // 4 - 1))
    mixed = jax.random.permutation(jax.random.fold_in(own, 3), amount)
    donor, sink = mixed[0:amount // 2 * 2:2], mixed[1:amount // 2 * 2:2]
    slack = jnp.minimum(tallies[donor] - 1, most - tallies[sink]) // 2
    slack = jnp.where((donor == ranking[0]) | (sink == ranking[0]) | (tallies[sink] == 0), 0, jnp.maximum(slack, 0))
    shifted = jax.random.randint(jax.random.fold_in(own, 4), (amount // 2,), 0, 1 << 20) % (slack + 1)
    tallies = tallies.at[donor].add(-shifted).at[sink].add(shifted)
    items = jnp.searchsorted(jnp.cumsum(tallies), jnp.arange(rows * top), side="right").astype(jnp.int32)
    listing = items.reshape(top, rows).T
    listing = listing[jax.random.permutation(jax.random.fold_in(own, 1), rows)]
    offset_by = jax.random.randint(jax.random.fold_in(own, 2), (rows, 1), 0, top)
    return jnp.take_along_axis(listing, (jnp.arange(top)[None, :] + offset_by) % top, axis=1)


def load_shares(amount, total, limit, slope, full):
    weights = [(1 << 20) // math.isqrt(grade ** slope) + 1 for grade in range(1, amount + 1)]
    largest = limit if full else min(limit, max(-(-total // amount), total * weights[0] // sum(weights)))
    least = 1 if total - largest >= amount - 1 else 0
    counts, rest = [largest] + [least] * (amount - 1), total - largest - least * (amount - 1)
    while rest > 0:
        candidates = [i for i in range(1, amount) if counts[i] < largest] or [i for i in range(1, amount) if counts[i] < limit]
        whole, remaining = sum([weights[i] for i in candidates]), rest
        for i in candidates:
            addition = min(limit - counts[i], max(1, remaining * weights[i] // whole), rest)
            counts[i] = counts[i] + addition
            rest = rest - addition
    return np.array(counts)


def setup_inputs(seed: int = 0) -> dict:
    splits = jax.random.split(jax.random.key(seed), 7)
    template = draw_template(jax.random.fold_in(splits[6], 71), 0)
    science = draw_science(jax.random.fold_in(splits[6], 71), 0)
    offsets = draw_offsets(jax.random.fold_in(splits[6], 71), 0)
    source_dest_keys = jax.random.split(jax.random.fold_in(splits[3], 1), SOURCES // NSRC)
    source_dest_turns = jax.random.permutation(jax.random.fold_in(splits[3], 3), SOURCES // NSRC)
    source_dest = jax.vmap(lambda own, number: routed_block(jax.random.fold_in(splits[3], 2), own, number, NSRC, DEVICES, 1, CAP, 2))(source_dest_keys, source_dest_turns).reshape((SOURCES, 1))
    source_row = touch_ends(jax.random.randint(splits[4], (SOURCES,), 0, ROWS - CUT + 1), jax.random.fold_in(splits[4], 1), 0, ROWS - CUT).astype(jnp.int32)
    source_col = touch_ends(jax.random.randint(splits[5], (SOURCES,), 0, COLS - CUT + 1), jax.random.fold_in(splits[5], 1), 0, COLS - CUT).astype(jnp.int32)
    return {"template": template, "science": science, "offsets": offsets, "source_dest": source_dest, "source_row": source_row, "source_col": source_col}


gauss_widths = (1.0, 2.5, 5.0)
ridge_scale = 0.02

def filter_bank():
    tap_axis = jnp.arange(2 * MARGIN + 1, dtype=jnp.float32) - MARGIN
    families = []
    for spread in gauss_widths:
        profile = jnp.exp(-tap_axis * tap_axis / (2.0 * spread * spread))
        profile = profile / jnp.sum(profile)
        scaled = tap_axis / spread
        families.append(jnp.stack([profile, profile * scaled, profile * scaled * scaled]))
    return jnp.stack(families)

def filter_rows(image, kernels):
    result = lax.conv_general_dilated(image[None, None], kernels[:, None, None, :], (1, 1), 'VALID', precision=lax.Precision.HIGHEST)
    return result[0]

def filter_cols(image, kernels):
    result = lax.conv_general_dilated(image[None, None], kernels[:, None, :, None], (1, 1), 'VALID', precision=lax.Precision.HIGHEST)
    return result[0]

def basis_images(window, filters):
    images = []
    for family in range(3):
        rowed = filter_rows(window, filters[family])
        for degree_x in range(3):
            images.append(filter_cols(rowed[degree_x], filters[family, :3 - degree_x]))
    return jnp.concatenate(images, 0)

def solve_weights(matrix, projection):
    count = matrix.shape[0]
    damped = matrix + ridge_scale * jnp.trace(matrix) / count * jnp.eye(count, dtype=matrix.dtype)
    factor = jnp.linalg.cholesky(damped)
    return jax.scipy.linalg.cho_solve((factor, True), projection)

def subtract_tile(window, observed, filters):
    basis = basis_images(window, filters).reshape(18, ROWS * COLS)
    regressors = jnp.concatenate([basis, jnp.ones_like(basis[:1])], 0)
    normal_matrix = lax.dot_general(regressors, regressors, (((1,), (1,)), ((), ())), precision=lax.Precision.HIGHEST)
    projection = jnp.dot(regressors, observed.reshape(-1), precision=lax.Precision.HIGHEST)
    coefficients = solve_weights(normal_matrix, projection)
    modelled = jnp.dot(coefficients, regressors, precision=lax.Precision.HIGHEST)
    return observed - modelled.reshape(ROWS, COLS)

def pack_stamps(difference, destination, top, left):
    stamps = jax.vmap(lambda top_row, left_col: lax.dynamic_slice(difference, (top_row, left_col), (CUT, CUT)))(top, left)
    stamps = stamps.reshape(NSRC, CUT * CUT).astype(jnp.bfloat16)
    dest_hot = (destination[:, None] == jnp.arange(DEVICES, dtype=jnp.int32)[None, :]).astype(jnp.int32)
    earlier = jnp.sum((jnp.cumsum(dest_hot, 0) - dest_hot) * dest_hot, 1)
    slot_index = (destination * CAP + earlier).astype(jnp.int32)
    buffer = jnp.zeros((DEVICES * CAP, CUT * CUT), jnp.bfloat16).at[slot_index].set(stamps)
    return buffer.reshape(DEVICES, CAP, CUT * CUT)

def reference(template, science, offsets, source_dest, source_row, source_col):
    filters = filter_bank()
    padded = jnp.pad(template, ((MARGIN, MARGIN), (0, 0)))
    padded = jnp.concatenate([padded[:, NX - MARGIN:], padded, padded[:, :OFFMAX + MARGIN]], 1)
    dest_all = source_dest[:, 0].reshape(N_RA * N_DEC, NSRC)
    rows_all = source_row.reshape(N_RA * N_DEC, NSRC)
    cols_all = source_col.reshape(N_RA * N_DEC, NSRC)

    def one_tile(tile_index):
        tile_ra = tile_index // N_DEC
        tile_dec = tile_index % N_DEC
        shift_cols = offsets[tile_ra, tile_dec]
        first_row = (tile_dec * ROWS).astype(jnp.int32)
        window = lax.dynamic_slice(padded, (first_row, (tile_ra * COLS + shift_cols).astype(jnp.int32)), (ROWS + 2 * MARGIN, COLS + 2 * MARGIN))
        observed = lax.dynamic_slice(science, (first_row, (tile_ra * COLS).astype(jnp.int32)), (ROWS, COLS))
        difference = subtract_tile(window, observed, filters)
        buffer = pack_stamps(difference, dest_all[tile_index], rows_all[tile_index], cols_all[tile_index])
        return (difference, buffer)
    tiles, buffers = lax.map(one_tile, jnp.arange(N_RA * N_DEC, dtype=jnp.int32))
    difference = tiles.reshape(N_RA, N_DEC, ROWS, COLS).transpose(1, 2, 0, 3).reshape(NY, NX)
    stamps = buffers.transpose(1, 0, 2, 3)
    return (difference, stamps)
```

```python
import functools

import jax
import jax.numpy as jnp
import ml_dtypes
import numpy as np
from jax import lax
from jax.experimental import pallas as pl
from jax.experimental.pallas import tpu as pltpu
from jax.sharding import PartitionSpec as P

MARGIN = 15
TAPS = 31
CUT = 64
CAP = 2
OFFMAX = 512
LANE = 128
EDGE = 16
RIGHT = 640
STEP = 96
DEEP = 128
GROUP = 16
COUNT = 19
MESH = pl.DeviceIdType.MESH

gauss_widths = (1.0, 2.5, 5.0)
ridge_scale = 0.02


def filter_bank():
    t = np.arange(TAPS, dtype=np.float64) - MARGIN
    rows = []
    for w in gauss_widths:
        p = np.exp(-t * t / (2.0 * w * w))
        p = p / p.sum()
        rows += [p, p * (t / w), p * (t / w) ** 2]
    return np.stack(rows)


def split16(x):
    hi = x.astype(np.float32).astype(ml_dtypes.bfloat16)
    lo = (x - hi.astype(np.float64)).astype(np.float32).astype(ml_dtypes.bfloat16)
    return hi, lo


def tables():
    f = filter_bank()
    p = np.arange(2 * LANE)[:, None]
    x = np.arange(LANE)[None, :]
    gap = p - x
    inside = (gap >= 0) & (gap < TAPS)
    picked = np.where(inside, np.clip(gap, 0, TAPS - 1), 0)
    wide = np.concatenate([np.where(inside, f[k][picked], 0.0) for k in range(9)], 1)
    hi, lo = split16(wide)
    across = np.concatenate([hi, hi, lo], 0)
    y = np.arange(STEP)[:, None]
    q = np.arange(DEEP)[None, :]
    gap = q - y - 1
    inside = (gap >= 0) & (gap < TAPS)
    picked = np.where(inside, np.clip(gap, 0, TAPS - 1), 0)
    tall = np.stack([np.where(inside, f[k][picked], 0.0) for k in range(9)], 0)
    hi, lo = split16(tall)
    return across, np.concatenate([hi, lo], 2), tall.astype(np.float32)


def halo_kernel(n_ra, n_dec, t_ref, out_ref, zero, ssem, rsem, lsem):
    r = lax.axis_index("ra")
    d = lax.axis_index("dec")
    rows, cols = t_ref.shape
    left = lax.rem(r + n_ra - 1, n_ra)
    right = lax.rem(r + 1, n_ra)
    barrier = pltpu.get_barrier_semaphore()
    has_up = d > 0
    has_down = d < n_dec - 1

    def greet(a, b):
        pl.semaphore_signal(barrier, inc=1, device_id={"ra": a, "dec": b}, device_id_type=MESH)

    greet(left, d)
    greet(right, d)

    @pl.when(has_up)
    def _():
        for a in (left, r, right):
            greet(a, d - 1)

    @pl.when(has_down)
    def _():
        for a in (left, r, right):
            greet(a, d + 1)

    zero[...] = jnp.zeros_like(zero)
    own = pltpu.make_async_copy(
        t_ref, out_ref.at[pl.ds(EDGE, rows), pl.ds(LANE, cols)], lsem.at[0]
    )
    own.start()
    blank_up = pltpu.make_async_copy(zero, out_ref.at[pl.ds(0, EDGE), :], lsem.at[1])
    blank_down = pltpu.make_async_copy(zero, out_ref.at[pl.ds(EDGE + rows, EDGE), :], lsem.at[2])

    @pl.when(jnp.logical_not(has_up))
    def _():
        blank_up.start()

    @pl.when(jnp.logical_not(has_down))
    def _():
        blank_down.start()

    peers = 2 + 3 * has_up.astype(jnp.int32) + 3 * has_down.astype(jnp.int32)
    pl.semaphore_wait(barrier, peers)

    spans = (
        (left, pl.ds(0, RIGHT), pl.ds(LANE + cols, RIGHT)),
        (r, pl.ds(0, cols), pl.ds(LANE, cols)),
        (right, pl.ds(cols - LANE, LANE), pl.ds(0, LANE)),
    )
    bands = (
        (d - 1, pl.ds(0, EDGE), pl.ds(EDGE + rows, EDGE)),
        (d, pl.ds(0, rows), pl.ds(EDGE, rows)),
        (d + 1, pl.ds(rows - EDGE, EDGE), pl.ds(0, EDGE)),
    )

    def copy(v, h):
        to_ra, c_src, c_dst = spans[h]
        to_dec, r_src, r_dst = bands[v]
        number = v * 3 + h
        return pltpu.make_async_remote_copy(
            src_ref=t_ref.at[r_src, c_src],
            dst_ref=out_ref.at[r_dst, c_dst],
            send_sem=ssem.at[number],
            recv_sem=rsem.at[number],
            device_id={"ra": to_ra, "dec": to_dec},
            device_id_type=MESH,
        )

    copy(1, 0).start()
    copy(1, 2).start()

    @pl.when(has_up)
    def _():
        for h in range(3):
            copy(0, h).start()

    @pl.when(has_down)
    def _():
        for h in range(3):
            copy(2, h).start()

    @pl.when(has_up)
    def _():
        for h in range(3):
            copy(0, h).wait_send()
            copy(2, h).wait_recv()

    @pl.when(has_down)
    def _():
        for h in range(3):
            copy(2, h).wait_send()
            copy(0, h).wait_recv()

    @pl.when(jnp.logical_not(has_up))
    def _():
        blank_up.wait()

    @pl.when(jnp.logical_not(has_down))
    def _():
        blank_down.wait()

    own.wait()
    copy(1, 2).wait()
    copy(1, 0).wait()


def halo(template, n_ra, n_dec):
    rows, cols = template.shape
    shape = (rows + 2 * EDGE, LANE + cols + RIGHT)
    return pl.pallas_call(
        functools.partial(halo_kernel, n_ra, n_dec),
        out_shape=jax.ShapeDtypeStruct(shape, jnp.float32),
        in_specs=[pl.BlockSpec(memory_space=pl.ANY)],
        out_specs=pl.BlockSpec(memory_space=pl.ANY),
        scratch_shapes=[
            pltpu.VMEM((EDGE, shape[1]), jnp.float32),
            pltpu.SemaphoreType.DMA((9,)),
            pltpu.SemaphoreType.DMA((9,)),
            pltpu.SemaphoreType.DMA((3,)),
        ],
        compiler_params=pltpu.CompilerParams(collective_id=0, has_side_effects=True),
        name="halo",
    )(template)


def tile_kernel(
    off_ref, dest_ref, row_ref, col_ref, joined, science, across, down2, down,
    diff_ref, out_ref,
    window, r_hi, r_lo, images, gram, padded, mix, tally,
):
    rows, cols = science.shape
    tall = rows + 2 * EDGE
    deep = r_hi.shape[1]
    sources = row_ref.shape[0]
    owners = out_ref.shape[0] // CAP
    blocks = cols // LANE
    f32, bf16 = jnp.float32, jnp.bfloat16

    start = LANE - MARGIN + off_ref[0, 0]
    base = start // LANE
    shift = start % LANE
    lane = lax.broadcasted_iota(jnp.int32, (tall, LANE), 1)

    def turned(c):
        at = pl.multiple_of((base + c) * LANE, LANE)
        return pltpu.roll(joined[:, pl.ds(at, LANE)], lax.rem(LANE - shift, LANE), 1)

    before = turned(0)
    for c in range(blocks + 1):
        after = turned(c + 1)
        value = jnp.where(lane < LANE - shift, before, after)
        hi = value.astype(bf16)
        window[0, :, c * LANE : (c + 1) * LANE] = hi
        window[1, :, c * LANE : (c + 1) * LANE] = (value - hi.astype(f32)).astype(bf16)
        before = after

    r_hi[:, tall:, :] = jnp.zeros((9, deep - tall, cols), bf16)
    r_lo[:, tall:, :] = jnp.zeros((9, deep - tall, cols), bf16)

    @pl.loop(0, blocks)
    def _(b):
        at = pl.multiple_of(b * LANE, LANE)
        hi = window[0, :, pl.ds(at, 2 * LANE)]
        lo = window[1, :, pl.ds(at, 2 * LANE)]
        left = jnp.concatenate([hi, lo, hi], 1)
        for g in range(3):
            product = jnp.dot(
                left, across[:, 3 * g * LANE : 3 * (g + 1) * LANE], preferred_element_type=f32
            )
            for i in range(3):
                part = product[:, i * LANE : (i + 1) * LANE]
                top = part.astype(bf16)
                r_hi[3 * g + i, 0:tall, pl.ds(at, LANE)] = top
                r_lo[3 * g + i, 0:tall, pl.ds(at, LANE)] = (part - top.astype(f32)).astype(bf16)

    gram[...] = jnp.zeros_like(gram)
    images[18] = jnp.ones((STEP, cols), bf16)
    chunk = min(cols, 2 * LANE)
    for y0 in range(0, rows, STEP):
        size = min(STEP, rows - y0)
        images[19, 0:size, :] = science[y0 : y0 + size, :].astype(bf16)

        @pl.loop(0, cols // chunk)
        def _(n):
            at = pl.multiple_of(n * chunk, chunk)
            k = 0
            for g in range(3):
                for i in range(3):
                    part = r_hi[3 * g + i, y0 : y0 + DEEP, pl.ds(at, chunk)]
                    count = 3 - i
                    left = down2[3 * g : 3 * g + count].reshape(count * STEP, 2 * DEEP)
                    product = jnp.dot(
                        left, jnp.concatenate([part, part], 0), preferred_element_type=f32
                    )
                    images[k : k + count, :, pl.ds(at, chunk)] = product.astype(bf16).reshape(
                        count, STEP, chunk
                    )
                    k = k + count

        @pl.loop(0, size // GROUP)
        def _(q):
            at = pl.multiple_of(q * GROUP, GROUP)
            stack = images[:, pl.ds(at, GROUP), :].reshape(20 * GROUP, cols)
            gram[...] += lax.dot_general(
                stack, stack, (((1,), (1,)), ((), ())), preferred_element_type=f32
            )

    length = 20 * GROUP
    ri = lax.broadcasted_iota(jnp.int32, (length, length), 0)
    ci = lax.broadcasted_iota(jnp.int32, (length, length), 1)
    kept = jnp.where(ri % GROUP == ci % GROUP, gram[...], 0.0)
    kept = jnp.sum(kept.reshape(20, GROUP, length), axis=1)
    pick = (
        lax.broadcasted_iota(jnp.int32, (length, LANE), 0) // GROUP
        == lax.broadcasted_iota(jnp.int32, (length, LANE), 1)
    ).astype(f32)
    system = jnp.dot(kept, pick, precision=lax.Precision.HIGHEST, preferred_element_type=f32)

    rr = lax.broadcasted_iota(jnp.int32, (20, LANE), 0)
    cc = lax.broadcasted_iota(jnp.int32, (20, LANE), 1)
    diagonal = (rr == cc) & (rr < COUNT)
    trace = jnp.sum(jnp.where(diagonal, system, 0.0), axis=(0, 1), keepdims=True)
    system = system + jnp.where(diagonal, ridge_scale * trace / COUNT, 0.0)
    for k in range(COUNT):
        pivot = system[k : k + 1, :] / system[k : k + 1, k : k + 1]
        system = jnp.where(rr == k, pivot, system - system[:, k : k + 1] * pivot)

    def weight(k):
        return system[k : k + 1, 19:20]

    k = 0
    for g in range(3):
        for i in range(3):
            total = jnp.zeros((STEP, DEEP), f32)
            for j in range(3 - i):
                total = total + weight(k) * down[3 * g + j]
                k = k + 1
            hi = total.astype(bf16)
            at = (3 * g + i) * DEEP
            mix[0:STEP, at : at + DEEP] = hi
            mix[STEP : 2 * STEP, at : at + DEEP] = (total - hi.astype(f32)).astype(bf16)
    flat = weight(18)

    for y0 in range(0, rows, STEP):
        size = min(STEP, rows - y0)

        for n in range(cols // chunk):
            at = n * chunk
            right = r_hi[:, y0 : y0 + DEEP, at : at + chunk].reshape(9 * DEEP, chunk)
            rest = r_lo[:, y0 : y0 + DEEP, at : at + chunk].reshape(9 * DEEP, chunk)
            both = jnp.dot(mix[...], right, preferred_element_type=f32)
            model = (
                both[0:STEP]
                + both[STEP:]
                + jnp.dot(mix[0:STEP, :], rest, preferred_element_type=f32)
            )
            value = science[y0 : y0 + size, at : at + chunk] - (model[0:size] + flat)
            diff_ref[y0 : y0 + size, at : at + chunk] = value
            for c in range(chunk // LANE):
                padded[at // LANE + c, y0 : y0 + size, :] = value[:, c * LANE : (c + 1) * LANE]

    out_ref[...] = jnp.zeros_like(out_ref)

    @pl.loop(0, owners)
    def _(e):
        tally[e] = 0

    lane2 = lax.broadcasted_iota(jnp.int32, (CUT // 2, LANE), 1)

    @pl.loop(0, sources)
    def _(n):
        owner = dest_ref[n, 0]
        slot = tally[owner]
        tally[owner] = slot + 1
        row = row_ref[n]
        col = col_ref[n]
        tile = col // LANE
        s = col % LANE
        first = lax.rem(LANE - s, LANE)
        second = lax.rem(LANE + CUT - s, LANE)

        def half(r0, turn, bound):
            a = pltpu.roll(padded[tile, pl.ds(r0, CUT // 2, stride=2), :], turn, 1)
            b = pltpu.roll(padded[tile + 1, pl.ds(r0, CUT // 2, stride=2), :], turn, 1)
            return jnp.where(lane2 < bound, a, b)

        even = half(row, first, LANE - s)
        odd = half(row + 1, second, LANE + CUT - s)
        stamp = jnp.where(lane2 < CUT, even, odd)
        out_ref[owner * CAP + slot] = stamp.astype(bf16)


def tile(joined, science, offsets, dest, row, col, devices):
    rows, cols = science.shape
    across, down2, down = tables()
    smem = pl.BlockSpec(memory_space=pltpu.SMEM)
    vmem = pl.BlockSpec(memory_space=pltpu.VMEM)
    deep = -(-rows // STEP) * STEP + DEEP - STEP
    bf16 = jnp.bfloat16
    return pl.pallas_call(
        tile_kernel,
        out_shape=(
            jax.ShapeDtypeStruct((rows, cols), jnp.float32),
            jax.ShapeDtypeStruct((devices * CAP, CUT // 2, LANE), bf16),
        ),
        in_specs=[smem] * 4 + [vmem] * 5,
        out_specs=(vmem, vmem),
        scratch_shapes=[
            pltpu.VMEM((2, rows + 2 * EDGE, cols + LANE), bf16),
            pltpu.VMEM((9, deep, cols), bf16),
            pltpu.VMEM((9, deep, cols), bf16),
            pltpu.VMEM((20, STEP, cols), bf16),
            pltpu.VMEM((20 * GROUP, 20 * GROUP), jnp.float32),
            pltpu.VMEM((cols // LANE + 1, rows, LANE), jnp.float32),
            pltpu.VMEM((2 * STEP, 9 * DEEP), bf16),
            pltpu.SMEM((devices,), jnp.int32),
        ],
        compiler_params=pltpu.CompilerParams(vmem_limit_bytes=52 * 1024 * 1024),
        name="tile",
    )(offsets, dest, row, col, joined, science, jnp.asarray(across), jnp.asarray(down2), jnp.asarray(down))


def exchange_kernel(n_ra, n_dec, in_ref, out_ref, ssem, rsem, lsem):
    me = lax.axis_index("ra") * n_dec + lax.axis_index("dec")
    devices = n_ra * n_dec
    barrier = pltpu.get_barrier_semaphore()

    def place(t):
        return {"ra": t // n_dec, "dec": t % n_dec}

    @pl.loop(1, devices)
    def _(k):
        pl.semaphore_signal(
            barrier, inc=1, device_id=place(lax.rem(me + k, devices)), device_id_type=MESH
        )

    own = pltpu.make_async_copy(in_ref.at[me], out_ref.at[me], lsem.at[0])
    own.start()
    pl.semaphore_wait(barrier, devices - 1)

    def copy(k, block):
        target = lax.rem(me + k, devices)
        return pltpu.make_async_remote_copy(
            src_ref=in_ref.at[target],
            dst_ref=out_ref.at[block],
            send_sem=ssem.at[k],
            recv_sem=rsem.at[k],
            device_id=place(target),
            device_id_type=MESH,
        )

    @pl.loop(1, devices)
    def _(k):
        copy(k, me).start()

    @pl.loop(1, devices)
    def _(k):
        copy(k, me).wait_send()
        copy(k, lax.rem(me + devices - k, devices)).wait_recv()

    own.wait()


def exchange(outgoing, n_ra, n_dec):
    devices = n_ra * n_dec
    return pl.pallas_call(
        functools.partial(exchange_kernel, n_ra, n_dec),
        out_shape=jax.ShapeDtypeStruct(outgoing.shape, outgoing.dtype),
        in_specs=[pl.BlockSpec(memory_space=pl.ANY)],
        out_specs=pl.BlockSpec(memory_space=pl.ANY),
        scratch_shapes=[
            pltpu.SemaphoreType.DMA((devices,)),
            pltpu.SemaphoreType.DMA((devices,)),
            pltpu.SemaphoreType.DMA((1,)),
        ],
        compiler_params=pltpu.CompilerParams(collective_id=1, has_side_effects=True),
        name="exchange",
    )(outgoing)


def solution(mesh):
    n_ra, n_dec = mesh.shape["ra"], mesh.shape["dec"]
    devices = n_ra * n_dec

    def per_device(template, science, offsets, source_dest, source_row, source_col):
        joined = halo(template, n_ra, n_dec)
        difference, outgoing = tile(
            joined, science, offsets, source_dest, source_row, source_col, devices
        )
        received = exchange(outgoing.reshape(devices, CAP, CUT // 2, LANE), n_ra, n_dec)
        return difference, received.reshape(1, devices, CAP, CUT * CUT)

    placed = (
        P("dec", "ra"),
        P("dec", "ra"),
        P("ra", "dec"),
        P(("ra", "dec"), None),
        P(("ra", "dec")),
        P(("ra", "dec")),
    )
    return jax.shard_map(
        per_device,
        mesh=mesh,
        in_specs=placed,
        out_specs=(P("dec", "ra"), P(("ra", "dec"), None, None, None)),
        check_vma=False,
    )
```

```python
import functools

import jax
import jax.numpy as jnp
import ml_dtypes
import numpy as np
from jax import lax
from jax.experimental import pallas as pl
from jax.experimental.pallas import tpu as pltpu
from jax.sharding import PartitionSpec as P

MARGIN = 15
TAPS = 31
CUT = 64
CAP = 2
OFFMAX = 512
LANE = 128
EDGE = 16
RIGHT = 640
STEP = 96
DEEP = 128
GROUP = 16
COUNT = 19
MESH = pl.DeviceIdType.MESH

gauss_widths = (1.0, 2.5, 5.0)
ridge_scale = 0.02


def filter_bank():
    t = np.arange(TAPS, dtype=np.float64) - MARGIN
    rows = []
    for w in gauss_widths:
        p = np.exp(-t * t / (2.0 * w * w))
        p = p / p.sum()
        rows += [p, p * (t / w), p * (t / w) ** 2]
    return np.stack(rows)


def split16(x):
    hi = x.astype(np.float32).astype(ml_dtypes.bfloat16)
    lo = (x - hi.astype(np.float64)).astype(np.float32).astype(ml_dtypes.bfloat16)
    return hi, lo


def tables():
    f = filter_bank()
    p = np.arange(2 * LANE)[:, None]
    x = np.arange(LANE)[None, :]
    gap = p - x
    inside = (gap >= 0) & (gap < TAPS)
    picked = np.where(inside, np.clip(gap, 0, TAPS - 1), 0)
    wide = np.concatenate([np.where(inside, f[k][picked], 0.0) for k in range(9)], 1)
    hi, lo = split16(wide)
    across = np.concatenate([hi, hi, lo], 0)
    y = np.arange(STEP)[:, None]
    q = np.arange(DEEP)[None, :]
    gap = q - y - 1
    inside = (gap >= 0) & (gap < TAPS)
    picked = np.where(inside, np.clip(gap, 0, TAPS - 1), 0)
    tall = np.stack([np.where(inside, f[k][picked], 0.0) for k in range(9)], 0)
    hi, lo = split16(tall)
    return across, np.concatenate([hi, lo], 2), tall.astype(np.float32)


def halo_kernel(n_ra, n_dec, t_ref, out_ref, zero, ssem, rsem, lsem):
    r = lax.axis_index("ra")
    d = lax.axis_index("dec")
    rows, cols = t_ref.shape
    left = lax.rem(r + n_ra - 1, n_ra)
    right = lax.rem(r + 1, n_ra)
    barrier = pltpu.get_barrier_semaphore()
    has_up = d > 0
    has_down = d < n_dec - 1

    def greet(a, b):
        pl.semaphore_signal(barrier, inc=1, device_id={"ra": a, "dec": b}, device_id_type=MESH)

    greet(left, d)
    greet(right, d)

    @pl.when(has_up)
    def _():
        for a in (left, r, right):
            greet(a, d - 1)

    @pl.when(has_down)
    def _():
        for a in (left, r, right):
            greet(a, d + 1)

    zero[...] = jnp.zeros_like(zero)
    blank_up = pltpu.make_async_copy(zero, out_ref.at[pl.ds(0, EDGE), :], lsem.at[0])
    blank_down = pltpu.make_async_copy(zero, out_ref.at[pl.ds(EDGE + rows, EDGE), :], lsem.at[1])

    @pl.when(jnp.logical_not(has_up))
    def _():
        blank_up.start()

    @pl.when(jnp.logical_not(has_down))
    def _():
        blank_down.start()

    peers = 2 + 3 * has_up.astype(jnp.int32) + 3 * has_down.astype(jnp.int32)
    pl.semaphore_wait(barrier, peers)

    spans = (
        (left, pl.ds(0, RIGHT), pl.ds(LANE + cols, RIGHT)),
        (r, pl.ds(0, cols), pl.ds(LANE, cols)),
        (right, pl.ds(cols - LANE, LANE), pl.ds(0, LANE)),
    )
    bands = (
        (d - 1, pl.ds(0, EDGE), pl.ds(EDGE + rows, EDGE)),
        (d, pl.ds(0, rows), pl.ds(EDGE, rows)),
        (d + 1, pl.ds(rows - EDGE, EDGE), pl.ds(0, EDGE)),
    )

    def copy(v, h):
        to_ra, c_src, c_dst = spans[h]
        to_dec, r_src, r_dst = bands[v]
        number = v * 3 + h
        return pltpu.make_async_remote_copy(
            src_ref=t_ref.at[r_src, c_src],
            dst_ref=out_ref.at[r_dst, c_dst],
            send_sem=ssem.at[number],
            recv_sem=rsem.at[number],
            device_id={"ra": to_ra, "dec": to_dec},
            device_id_type=MESH,
        )

    copy(1, 0).start()
    copy(1, 2).start()

    @pl.when(has_up)
    def _():
        for h in range(3):
            copy(0, h).start()

    @pl.when(has_down)
    def _():
        for h in range(3):
            copy(2, h).start()

    @pl.when(has_up)
    def _():
        for h in range(3):
            copy(0, h).wait_send()
            copy(2, h).wait_recv()

    @pl.when(has_down)
    def _():
        for h in range(3):
            copy(2, h).wait_send()
            copy(0, h).wait_recv()

    @pl.when(jnp.logical_not(has_up))
    def _():
        blank_up.wait()

    @pl.when(jnp.logical_not(has_down))
    def _():
        blank_down.wait()

    copy(1, 2).wait()
    copy(1, 0).wait()


def halo(template, n_ra, n_dec):
    rows, cols = template.shape
    shape = (rows + 2 * EDGE, LANE + cols + RIGHT)
    return pl.pallas_call(
        functools.partial(halo_kernel, n_ra, n_dec),
        out_shape=jax.ShapeDtypeStruct(shape, jnp.float32),
        in_specs=[pl.BlockSpec(memory_space=pl.ANY)],
        out_specs=pl.BlockSpec(memory_space=pl.ANY),
        scratch_shapes=[
            pltpu.VMEM((EDGE, shape[1]), jnp.float32),
            pltpu.SemaphoreType.DMA((9,)),
            pltpu.SemaphoreType.DMA((9,)),
            pltpu.SemaphoreType.DMA((2,)),
        ],
        compiler_params=pltpu.CompilerParams(collective_id=0, has_side_effects=True),
        name="halo",
    )(template)


def tile_kernel(
    off_ref, dest_ref, row_ref, col_ref, template_in, edges_in, science_in, across_in, down2_in, down_in,
    diff_out, out_ref,
    joined, science, across, down2, down, diff_ref, sems, window, r_hi, r_lo, images, gram, padded, mix, tally,
):
    rows, cols = science.shape
    tall = rows + 2 * EDGE
    fetches = []

    def fetch(src, dst):
        fetches.append(pltpu.make_async_copy(src, dst, sems.at[len(fetches)]))
        fetches[-1].start()

    middle = slice(EDGE, EDGE + rows)
    fetch(template_in, joined.at[middle, LANE : LANE + cols])
    fetch(edges_in.at[middle, LANE + cols :], joined.at[middle, LANE + cols :])
    fetch(edges_in.at[middle, 0:LANE], joined.at[middle, 0:LANE])
    fetch(edges_in.at[0:EDGE, :], joined.at[0:EDGE, :])
    fetch(edges_in.at[EDGE + rows :, :], joined.at[EDGE + rows :, :])
    fetch(across_in, across)
    fetch(science_in, science)
    fetch(down2_in, down2)
    fetch(down_in, down)
    for k in range(5):
        fetches[k].wait()
    deep = r_hi.shape[1]
    sources = row_ref.shape[0]
    owners = out_ref.shape[0] // CAP
    blocks = cols // LANE
    f32, bf16 = jnp.float32, jnp.bfloat16

    start = LANE - MARGIN + off_ref[0, 0]
    base = start // LANE
    shift = start % LANE
    lane = lax.broadcasted_iota(jnp.int32, (tall, LANE), 1)

    def turned(c):
        at = pl.multiple_of((base + c) * LANE, LANE)
        return pltpu.roll(joined[:, pl.ds(at, LANE)], lax.rem(LANE - shift, LANE), 1)

    before = turned(0)
    for c in range(blocks + 1):
        after = turned(c + 1)
        value = jnp.where(lane < LANE - shift, before, after)
        hi = value.astype(bf16)
        window[0, :, c * LANE : (c + 1) * LANE] = hi
        window[1, :, c * LANE : (c + 1) * LANE] = (value - hi.astype(f32)).astype(bf16)
        before = after

    r_hi[:, tall:, :] = jnp.zeros((9, deep - tall, cols), bf16)
    r_lo[:, tall:, :] = jnp.zeros((9, deep - tall, cols), bf16)

    fetches[5].wait()

    @pl.loop(0, blocks)
    def _(b):
        at = pl.multiple_of(b * LANE, LANE)
        hi = window[0, :, pl.ds(at, 2 * LANE)]
        lo = window[1, :, pl.ds(at, 2 * LANE)]
        left = jnp.concatenate([hi, lo, hi], 1)
        for g in range(3):
            product = jnp.dot(
                left, across[:, 3 * g * LANE : 3 * (g + 1) * LANE], preferred_element_type=f32
            )
            for i in range(3):
                part = product[:, i * LANE : (i + 1) * LANE]
                top = part.astype(bf16)
                r_hi[3 * g + i, 0:tall, pl.ds(at, LANE)] = top
                r_lo[3 * g + i, 0:tall, pl.ds(at, LANE)] = (part - top.astype(f32)).astype(bf16)

    for k in range(6, 9):
        fetches[k].wait()
    gram[...] = jnp.zeros_like(gram)
    images[18] = jnp.ones((STEP, cols), bf16)
    chunk = min(cols, 2 * LANE)
    for y0 in range(0, rows, STEP):
        size = min(STEP, rows - y0)
        images[19, 0:size, :] = science[y0 : y0 + size, :].astype(bf16)

        @pl.loop(0, cols // chunk)
        def _(n):
            at = pl.multiple_of(n * chunk, chunk)
            k = 0
            for g in range(3):
                for i in range(3):
                    part = r_hi[3 * g + i, y0 : y0 + DEEP, pl.ds(at, chunk)]
                    count = 3 - i
                    left = down2[3 * g : 3 * g + count].reshape(count * STEP, 2 * DEEP)
                    product = jnp.dot(
                        left, jnp.concatenate([part, part], 0), preferred_element_type=f32
                    )
                    images[k : k + count, :, pl.ds(at, chunk)] = product.astype(bf16).reshape(
                        count, STEP, chunk
                    )
                    k = k + count

        @pl.loop(0, size // GROUP)
        def _(q):
            at = pl.multiple_of(q * GROUP, GROUP)
            stack = images[:, pl.ds(at, GROUP), :].reshape(20 * GROUP, cols)
            gram[...] += lax.dot_general(
                stack, stack, (((1,), (1,)), ((), ())), preferred_element_type=f32
            )

    length = 20 * GROUP
    ri = lax.broadcasted_iota(jnp.int32, (length, length), 0)
    ci = lax.broadcasted_iota(jnp.int32, (length, length), 1)
    kept = jnp.where(ri % GROUP == ci % GROUP, gram[...], 0.0)
    kept = jnp.sum(kept.reshape(20, GROUP, length), axis=1)
    pick = (
        lax.broadcasted_iota(jnp.int32, (length, LANE), 0) // GROUP
        == lax.broadcasted_iota(jnp.int32, (length, LANE), 1)
    ).astype(f32)
    system = jnp.dot(kept, pick, precision=lax.Precision.HIGHEST, preferred_element_type=f32)

    rr = lax.broadcasted_iota(jnp.int32, (20, LANE), 0)
    cc = lax.broadcasted_iota(jnp.int32, (20, LANE), 1)
    diagonal = (rr == cc) & (rr < COUNT)
    trace = jnp.sum(jnp.where(diagonal, system, 0.0), axis=(0, 1), keepdims=True)
    system = system + jnp.where(diagonal, ridge_scale * trace / COUNT, 0.0)
    for k in range(COUNT):
        pivot = system[k : k + 1, :] / system[k : k + 1, k : k + 1]
        system = jnp.where(rr == k, pivot, system - system[:, k : k + 1] * pivot)

    def weight(k):
        return system[k : k + 1, 19:20]

    k = 0
    for g in range(3):
        for i in range(3):
            total = jnp.zeros((STEP, DEEP), f32)
            for j in range(3 - i):
                total = total + weight(k) * down[3 * g + j]
                k = k + 1
            hi = total.astype(bf16)
            at = (3 * g + i) * DEEP
            mix[0:STEP, at : at + DEEP] = hi
            mix[STEP : 2 * STEP, at : at + DEEP] = (total - hi.astype(f32)).astype(bf16)
    flat = weight(18)

    stores = []
    for y0 in range(0, rows, STEP):
        size = min(STEP, rows - y0)

        for n in range(cols // chunk):
            at = n * chunk
            right = r_hi[:, y0 : y0 + DEEP, at : at + chunk].reshape(9 * DEEP, chunk)
            rest = r_lo[:, y0 : y0 + DEEP, at : at + chunk].reshape(9 * DEEP, chunk)
            both = jnp.dot(mix[...], right, preferred_element_type=f32)
            model = (
                both[0:STEP]
                + both[STEP:]
                + jnp.dot(mix[0:STEP, :], rest, preferred_element_type=f32)
            )
            value = science[y0 : y0 + size, at : at + chunk] - (model[0:size] + flat)
            diff_ref[y0 : y0 + size, at : at + chunk] = value
            for c in range(chunk // LANE):
                padded[at // LANE + c, y0 : y0 + size, :] = value[:, c * LANE : (c + 1) * LANE]

        span = slice(y0, y0 + size)
        stores.append(
            pltpu.make_async_copy(diff_ref.at[span], diff_out.at[span], sems.at[9 + len(stores)])
        )
        stores[-1].start()

    out_ref[...] = jnp.zeros_like(out_ref)

    @pl.loop(0, owners)
    def _(e):
        tally[e] = 0

    lane2 = lax.broadcasted_iota(jnp.int32, (CUT // 2, LANE), 1)

    @pl.loop(0, sources)
    def _(n):
        owner = dest_ref[n, 0]
        slot = tally[owner]
        tally[owner] = slot + 1
        row = row_ref[n]
        col = col_ref[n]
        tile = col // LANE
        s = col % LANE
        first = lax.rem(LANE - s, LANE)
        second = lax.rem(LANE + CUT - s, LANE)

        def half(r0, turn, bound):
            a = pltpu.roll(padded[tile, pl.ds(r0, CUT // 2, stride=2), :], turn, 1)
            b = pltpu.roll(padded[tile + 1, pl.ds(r0, CUT // 2, stride=2), :], turn, 1)
            return jnp.where(lane2 < bound, a, b)

        even = half(row, first, LANE - s)
        odd = half(row + 1, second, LANE + CUT - s)
        stamp = jnp.where(lane2 < CUT, even, odd)
        out_ref[owner * CAP + slot] = stamp.astype(bf16)

    for store in stores:
        store.wait()


def tile(template, edges, science, offsets, dest, row, col, devices):
    rows, cols = science.shape
    across, down2, down = tables()
    smem = pl.BlockSpec(memory_space=pltpu.SMEM)
    vmem = pl.BlockSpec(memory_space=pltpu.VMEM)
    hbm = pl.BlockSpec(memory_space=pl.ANY)
    deep = -(-rows // STEP) * STEP + DEEP - STEP
    bf16 = jnp.bfloat16
    return pl.pallas_call(
        tile_kernel,
        out_shape=(
            jax.ShapeDtypeStruct((rows, cols), jnp.float32),
            jax.ShapeDtypeStruct((devices * CAP, CUT // 2, LANE), bf16),
        ),
        in_specs=[smem] * 4 + [hbm] * 6,
        out_specs=(hbm, vmem),
        scratch_shapes=[
            pltpu.VMEM(edges.shape, jnp.float32),
            pltpu.VMEM((rows, cols), jnp.float32),
            pltpu.VMEM(across.shape, bf16),
            pltpu.VMEM(down2.shape, bf16),
            pltpu.VMEM(down.shape, jnp.float32),
            pltpu.VMEM((rows, cols), jnp.float32),
            pltpu.SemaphoreType.DMA((9 + -(-rows // STEP),)),
            pltpu.VMEM((2, rows + 2 * EDGE, cols + LANE), bf16),
            pltpu.VMEM((9, deep, cols), bf16),
            pltpu.VMEM((9, deep, cols), bf16),
            pltpu.VMEM((20, STEP, cols), bf16),
            pltpu.VMEM((20 * GROUP, 20 * GROUP), jnp.float32),
            pltpu.VMEM((cols // LANE + 1, rows, LANE), jnp.float32),
            pltpu.VMEM((2 * STEP, 9 * DEEP), bf16),
            pltpu.SMEM((devices,), jnp.int32),
        ],
        compiler_params=pltpu.CompilerParams(vmem_limit_bytes=52 * 1024 * 1024),
        name="tile",
    )(offsets, dest, row, col, template, edges, science, jnp.asarray(across), jnp.asarray(down2), jnp.asarray(down))


def exchange_kernel(n_ra, n_dec, in_ref, out_ref, ssem, rsem, lsem):
    me = lax.axis_index("ra") * n_dec + lax.axis_index("dec")
    devices = n_ra * n_dec
    barrier = pltpu.get_barrier_semaphore()

    def place(t):
        return {"ra": t // n_dec, "dec": t % n_dec}

    @pl.loop(1, devices)
    def _(k):
        pl.semaphore_signal(
            barrier, inc=1, device_id=place(lax.rem(me + k, devices)), device_id_type=MESH
        )

    own = pltpu.make_async_copy(in_ref.at[me], out_ref.at[me], lsem.at[0])
    own.start()
    pl.semaphore_wait(barrier, devices - 1)

    def copy(k, block):
        target = lax.rem(me + k, devices)
        return pltpu.make_async_remote_copy(
            src_ref=in_ref.at[target],
            dst_ref=out_ref.at[block],
            send_sem=ssem.at[k],
            recv_sem=rsem.at[k],
            device_id=place(target),
            device_id_type=MESH,
        )

    @pl.loop(1, devices)
    def _(k):
        copy(k, me).start()

    @pl.loop(1, devices)
    def _(k):
        copy(k, me).wait_send()
        copy(k, lax.rem(me + devices - k, devices)).wait_recv()

    own.wait()


def exchange(outgoing, n_ra, n_dec):
    devices = n_ra * n_dec
    return pl.pallas_call(
        functools.partial(exchange_kernel, n_ra, n_dec),
        out_shape=jax.ShapeDtypeStruct(outgoing.shape, outgoing.dtype),
        in_specs=[pl.BlockSpec(memory_space=pl.ANY)],
        out_specs=pl.BlockSpec(memory_space=pl.ANY),
        scratch_shapes=[
            pltpu.SemaphoreType.DMA((devices,)),
            pltpu.SemaphoreType.DMA((devices,)),
            pltpu.SemaphoreType.DMA((1,)),
        ],
        compiler_params=pltpu.CompilerParams(collective_id=1, has_side_effects=True),
        name="exchange",
    )(outgoing)


def solution(mesh):
    n_ra, n_dec = mesh.shape["ra"], mesh.shape["dec"]
    devices = n_ra * n_dec

    def per_device(template, science, offsets, source_dest, source_row, source_col):
        edges = halo(template, n_ra, n_dec)
        difference, outgoing = tile(
            template, edges, science, offsets, source_dest, source_row, source_col, devices
        )
        received = exchange(outgoing.reshape(devices, CAP, CUT // 2, LANE), n_ra, n_dec)
        return difference, received.reshape(1, devices, CAP, CUT * CUT)

    placed = (
        P("dec", "ra"),
        P("dec", "ra"),
        P("ra", "dec"),
        P(("ra", "dec"), None),
        P(("ra", "dec")),
        P(("ra", "dec")),
    )
    return jax.shard_map(
        per_device,
        mesh=mesh,
        in_specs=placed,
        out_specs=(P("dec", "ra"), P(("ra", "dec"), None, None, None)),
        check_vma=False,
    )
```
